512 devices in a mesh: dp: 32 (over z_lo, y, core), ctx: 16 (over z_hi, x).
Axes of the slice: x: 4, y: 4, z: 16 (z_hi: 4, z_lo: 4; z = z_hi * 4 + z_lo), core: 2. Of those that a mesh axis runs over, the one named last changes fastest.
Arguments:
- tokens: bfloat16 [65536, 2048], P(('dp', 'ctx')), may hold values from -6 to 6
- out_grad: bfloat16 [65536, 2048], P(('dp', 'ctx')), may hold values from -6 to 6
- routes: int32 [65536, 2], P(('dp', 'ctx')), may hold values from 0 to 15, all different within a row; in each aligned block of 128 rows (0 to 127, 128 to 255, ...) at most 20 rows name the same one
- route_probs: float32 [65536, 2], P(('dp', 'ctx')), may hold values from 0.1 to 1
- gate_weight: bfloat16 [16, 2048, 768], P('ctx', 'dp'), may hold values from -0.125 to 0.125
- up_weight: bfloat16 [16, 2048, 768], P('ctx', 'dp'), may hold values from -0.125 to 0.125
- down_weight: bfloat16 [16, 768, 2048], P('ctx', 'dp'), may hold values from -0.21875 to 0.21875
Outputs:
- token_grad: bfloat16 [65536, 2048], P(('dp', 'ctx'))
- down_grad: float32 [16, 768, 2048], P('ctx', 'dp')
The draws below stay inside these ranges and needn't reach their ends.
Inputs may be any that keep to these rules, and one draw needn't show every extreme that they name: Within the 128 tokens of one device no expert is named by more than 20 routes, a bound that some block reaches.
All inputs are finite; a program needn't handle non-finite values.
Results may differ from the reference program's by a relative error of at most 0.029.
Values may be sent and summed in bfloat16 or wider, within the bound.
No kernel may reach another device: no remote copies, remote signals or barrier semaphores. Data moves between devices by JAX's collectives and lax.ppermute only.
A program may use at most 64 MiB of HBM per device.

```python
import math
import jax
import jax.numpy as jnp
import numpy as np
from jax import lax

D = 2048
H = 768
K = 2
TOK_DEV = 128
E = 16
C = 20
TOKENS = 65536
N_DP = 32
N_CTX = 16


def block_levels(stream_key, shape, cuts, least, top_value):
    level, own = 1.0, jax.random.fold_in(stream_key, 6)
    for axis_at, parts in cuts:
        steps = jnp.exp(jax.random.uniform(jax.random.fold_in(own, axis_at), (parts,), jnp.float32, least / len(cuts), top_value / len(cuts)))
        level = level * jnp.repeat(steps, shape[axis_at] // parts).reshape([-1 if axis == axis_at else 1 for axis in range(len(shape))])
    return level


def shared_out(key, own, number, rows, number_of, top, reach, skew):
    sequence = jax.random.permutation(key, number_of)
    heavy_load, common = portions_of(number_of, rows * top, reach, skew, True), portions_of(number_of, rows * top, reach, skew, False)
    places = jnp.arange(number_of)

    def named(tallies, rotation):
        used = int((tallies > 0).sum())
        fixed = max(1, used // 4)
        passed = fixed + (places - fixed + rotation * (used - fixed)) % max(1, number_of - fixed)
        return jnp.zeros((number_of,), jnp.int32).at[sequence[jnp.where(places < fixed, places, passed)]].set(jnp.asarray(tallies, jnp.int32))

    tallies = jnp.where(number % 4 == 0, named(heavy_load, number // 4), named(common, number - number // 4 - 1))
    mixed = jax.random.permutation(jax.random.fold_in(own, 3), number_of)
    giver, sink = mixed[0:number_of // 2 * 2:2], mixed[1:number_of // 2 * 2:2]
    margin = jnp.minimum(tallies[giver] - 1, reach - tallies[sink]) // 2
    margin = jnp.where((giver == sequence[0]) | (sink == sequence[0]) | (tallies[sink] == 0), 0, jnp.maximum(margin, 0))
    passed = jax.random.randint(jax.random.fold_in(own, 4), (number_of // 2,), 0, 1 << 20) % (margin + 1)
    tallies = tallies.at[giver].add(-passed).at[sink].add(passed)
    members = jnp.searchsorted(jnp.cumsum(tallies), jnp.arange(rows * top), side="right").astype(jnp.int32)
    table = members.reshape(top, rows).T
    table = table[jax.random.permutation(jax.random.fold_in(own, 1), rows)]
    rotation = jax.random.randint(jax.random.fold_in(own, 2), (rows, 1), 0, top)
    return jnp.take_along_axis(table, (jnp.arange(top)[None, :] + rotation) % top, axis=1)


def portions_of(amount, total, bound, slope, full):
    loads = [(1 << 20) // math.isqrt(grade ** slope) + 1 for grade in range(1, amount + 1)]
    largest = bound if full else min(bound, max(-(-total // amount), total * loads[0] // sum(loads)))
    least = 1 if total - largest >= amount - 1 else 0
    given, spare = [largest] + [least] * (amount - 1), total - largest - least * (amount - 1)
    while spare > 0:
        free = [i for i in range(1, amount) if given[i] < largest] or [i for i in range(1, amount) if given[i] < bound]
        whole, remaining = sum([loads[i] for i in free]), spare
        for i in free:
            extra = min(bound - given[i], max(1, remaining * loads[i] // whole), spare)
            given[i] = given[i] + extra
            spare = spare - extra
    return np.array(given)


def bell_draw(own_key, dims, deviation, limit, shards=(), kind=jnp.bfloat16):
    gain = block_levels(own_key, dims, shards, -0.22, 0.18) if shards else 1.0
    values = jax.random.normal(own_key, dims, jnp.float32) * deviation * gain
    return jnp.minimum(jnp.maximum(values, -limit), limit).astype(kind)


def setup_inputs(seed: int = 0) -> dict:
    seeds = jax.random.split(jax.random.key(seed), 8)
    tokens = bell_draw(seeds[0], (TOKENS, D), 1.0, 6.0, ((0, 512),))
    out_grad = bell_draw(seeds[1], (TOKENS, D), 1.0, 6.0, ((0, 512),))
    routes_keys = jax.random.split(jax.random.fold_in(seeds[2], 1), TOKENS // TOK_DEV)
    routes_turns = jax.random.permutation(jax.random.fold_in(seeds[2], 3), TOKENS // TOK_DEV)
    routes = jax.vmap(lambda own, number: shared_out(jax.random.fold_in(seeds[2], 2), own, number, TOK_DEV, E, K, C, 2))(routes_keys, routes_turns).reshape((TOKENS, K))
    route_probs = jnp.clip(jnp.exp(math.log(1.0) - 2.3025851 * jax.random.uniform(seeds[3], (TOKENS, K), jnp.float32) ** block_levels(seeds[3], (TOKENS, K), ((0, 512),), -0.2, 0.2)), 0.1, 1.0)
    gate_weight = bell_draw(seeds[4], (E, D, H), D ** -0.5, 0.125, ((0, 16), (1, 32)))
    up_weight = bell_draw(seeds[5], (E, D, H), D ** -0.5, 0.125, ((0, 16), (1, 32)))
    down_weight = bell_draw(seeds[6], (E, H, D), H ** -0.5, 0.21875, ((0, 16), (1, 32)))
    return {"tokens": tokens, "out_grad": out_grad, "routes": routes, "route_probs": route_probs, "gate_weight": gate_weight, "up_weight": up_weight, "down_weight": down_weight}


def expert_backward(token_rows, grad_rows, gate_mat, up_mat, down_mat):
    gate_pre = jnp.dot(token_rows, gate_mat, preferred_element_type=jnp.float32)
    up_pre = jnp.dot(token_rows, up_mat, preferred_element_type=jnp.float32)
    sigmoid_gate = jax.nn.sigmoid(gate_pre)
    hidden = (gate_pre * sigmoid_gate * up_pre).astype(jnp.bfloat16)
    hidden_grad = jnp.dot(grad_rows, down_mat.T, preferred_element_type=jnp.float32)
    gate_grad = (hidden_grad * up_pre * sigmoid_gate * (1.0 + gate_pre * (1.0 - sigmoid_gate))).astype(jnp.bfloat16)
    up_grad = (hidden_grad * gate_pre * sigmoid_gate).astype(jnp.bfloat16)
    input_grad = jnp.dot(gate_grad, gate_mat.T, preferred_element_type=jnp.float32)
    input_grad = (input_grad + jnp.dot(up_grad, up_mat.T, preferred_element_type=jnp.float32)).astype(jnp.bfloat16)
    weight_grad = jnp.dot(hidden.T, grad_rows, preferred_element_type=jnp.float32)
    return input_grad, weight_grad


def group_backward(token_group, grad_group, route_group, prob_group, gate_weight, up_weight, down_weight):
    experts = N_CTX
    route_count = TOK_DEV * K
    flat_routes = route_group.reshape(N_CTX, route_count).astype(jnp.int32)
    onehot = (flat_routes[:, :, None] == jnp.arange(experts, dtype=jnp.int32)[None, None, :]).astype(jnp.int32)
    slot_index = jnp.sum((jnp.cumsum(onehot, axis=1) - onehot) * onehot, axis=2)
    source = jnp.arange(N_CTX, dtype=jnp.int32)[:, None]
    target = ((flat_routes * N_CTX + source) * C + slot_index).reshape(-1).astype(jnp.int32)
    token_rows = jnp.repeat(token_group, K, axis=0)
    grad_rows = (prob_group.reshape(-1)[:, None] * jnp.repeat(grad_group, K, axis=0).astype(jnp.float32)).astype(jnp.bfloat16)
    slots = experts * N_CTX * C
    token_buffer = jnp.zeros((slots, D), jnp.bfloat16).at[target].set(token_rows).reshape(experts, N_CTX * C, D)
    grad_buffer = jnp.zeros((slots, D), jnp.bfloat16).at[target].set(grad_rows).reshape(experts, N_CTX * C, D)

    def per_expert(operands):
        return expert_backward(*operands)

    input_grad, weight_grad = lax.map(per_expert, (token_buffer, grad_buffer, gate_weight, up_weight, down_weight))
    row_grads = input_grad.reshape(slots, D)[target]
    token_grad = jnp.sum(row_grads.astype(jnp.float32).reshape(N_CTX * TOK_DEV, K, D), axis=1).astype(jnp.bfloat16)
    return token_grad, weight_grad.astype(jnp.bfloat16)


def reference(tokens, out_grad, routes, route_probs, gate_weight, up_weight, down_weight):
    token_groups = tokens.reshape(N_DP, N_CTX * TOK_DEV, D)
    grad_groups = out_grad.reshape(N_DP, N_CTX * TOK_DEV, D)
    route_groups = routes.reshape(N_DP, N_CTX * TOK_DEV, K)
    prob_groups = route_probs.reshape(N_DP, N_CTX * TOK_DEV, K)

    def step(total, operands):
        token_grad, weight_grad = group_backward(operands[0], operands[1], operands[2], operands[3], gate_weight, up_weight, down_weight)
        return total + weight_grad.astype(jnp.float32), token_grad

    down_total, token_grads = lax.scan(step, jnp.zeros((N_CTX, H, D), jnp.float32), (token_groups, grad_groups, route_groups, prob_groups))
    return token_grads.reshape(TOKENS, D), down_total
```

```python
import jax
import jax.numpy as jnp
from jax import lax
from jax.sharding import Mesh, PartitionSpec as P

AXES = ("zl", "y", "core", "zh", "x")
SIZES = (4, 4, 2, 4, 4)
PLANE = ("y", "x")
COLUMN = ("zl", "zh", "core")
SWAP = [(a * 4 + b, b * 4 + a) for a in range(4) for b in range(4)]


def swap(block):
    return lax.ppermute(block, ("y", "zh"), SWAP)


def shards(tokens, out_grad, routes, route_probs, gate_weight, up_weight, down_weight):
    tok_count, model_width = tokens.shape
    top_count = routes.shape[1]
    experts = lax.axis_size("y") * lax.axis_size("x")
    capacity = tok_count * top_count * 5 // (4 * experts)
    route_count = tok_count * top_count
    flat_routes = routes.reshape(route_count)
    onehot = (flat_routes[:, None] == jnp.arange(experts, dtype=jnp.int32)[None, :]).astype(
        jnp.int32
    )
    slot_index = jnp.sum((jnp.cumsum(onehot, axis=0) - onehot) * onehot, axis=1)
    target = flat_routes * capacity + slot_index
    token_rows = jnp.repeat(tokens, top_count, axis=0)
    grad_rows = (
        route_probs.reshape(route_count)[:, None]
        * jnp.repeat(out_grad, top_count, axis=0).astype(jnp.float32)
    ).astype(jnp.bfloat16)
    token_buffer = (
        jnp.zeros((experts * capacity, model_width), jnp.bfloat16).at[target].set(token_rows)
    )
    grad_buffer = (
        jnp.zeros((experts * capacity, model_width), jnp.bfloat16).at[target].set(grad_rows)
    )
    token_recv, grad_recv = (
        lax.all_to_all(
            token_buffer.reshape(experts, capacity, model_width),
            PLANE,
            split_axis=0,
            concat_axis=0,
            tiled=True,
        ),
        lax.all_to_all(
            grad_buffer.reshape(experts, capacity, model_width),
            PLANE,
            split_axis=0,
            concat_axis=0,
            tiled=True,
        ),
    )
    token_in = token_recv.reshape(experts * capacity, model_width)
    grad_in = grad_recv.reshape(experts * capacity, model_width)
    gate_full, up_full, down_full = (
        lax.all_gather(swap(gate_weight), COLUMN, axis=1, tiled=True),
        lax.all_gather(swap(up_weight), COLUMN, axis=1, tiled=True),
        lax.all_gather(swap(down_weight), COLUMN, axis=1, tiled=True),
    )
    gate_mat = gate_full[0]
    up_mat = up_full[0]
    gate_pre = jnp.dot(token_in, gate_mat, preferred_element_type=jnp.float32)
    up_pre = jnp.dot(token_in, up_mat, preferred_element_type=jnp.float32)
    hidden_grad = lax.dot_general(
        grad_in, down_full[0], (((1,), (1,)), ((), ())), preferred_element_type=jnp.float32
    )
    sigmoid_gate = jax.nn.sigmoid(gate_pre)
    hidden = (gate_pre * sigmoid_gate * up_pre).astype(jnp.bfloat16)
    gate_grad = (
        hidden_grad * up_pre * sigmoid_gate * (1.0 + gate_pre * (1.0 - sigmoid_gate))
    ).astype(jnp.bfloat16)
    up_grad = (hidden_grad * gate_pre * sigmoid_gate).astype(jnp.bfloat16)
    input_grad = lax.dot_general(
        gate_grad, gate_mat, (((1,), (1,)), ((), ())), preferred_element_type=jnp.float32
    )
    input_grad = input_grad + lax.dot_general(
        up_grad, up_mat, (((1,), (1,)), ((), ())), preferred_element_type=jnp.float32
    )
    input_grad = input_grad.astype(jnp.bfloat16)
    weight_term = lax.dot_general(
        hidden, grad_in, (((0,), (0,)), ((), ())), preferred_element_type=jnp.float32
    )
    shard_grad = swap(
        lax.psum_scatter(
            weight_term.astype(jnp.bfloat16), COLUMN, scatter_dimension=0, tiled=True
        )
    ).astype(jnp.float32)
    returned = lax.all_to_all(
        input_grad.reshape(experts, capacity, model_width),
        PLANE,
        split_axis=0,
        concat_axis=0,
        tiled=True,
    )
    route_grads = returned.reshape(experts * capacity, model_width)[target]
    token_grad = jnp.sum(
        route_grads.astype(jnp.float32).reshape(tok_count, top_count, model_width), axis=1
    ).astype(jnp.bfloat16)
    return (token_grad, shard_grad[None])


def solution(mesh):
    fine = Mesh(mesh.devices.reshape(SIZES), AXES)
    rows, experts, parts = AXES, ("zh", "x"), ("zl", "y", "core")
    in_specs = (
        P(rows, None),
        P(rows, None),
        P(rows, None),
        P(rows, None),
        P(experts, parts, None),
        P(experts, parts, None),
        P(experts, parts, None),
    )
    out_specs = (P(rows, None), P(experts, parts, None))
    return jax.shard_map(shards, mesh=fine, in_specs=in_specs, out_specs=out_specs, check_vma=False)
```

```python
import jax
import jax.numpy as jnp
from jax import lax
from jax.sharding import Mesh, PartitionSpec as P

AXES = ("zl", "y", "core", "zh", "x")
SIZES = (4, 4, 2, 4, 4)
SWAP_CORES = [(0, 1), (1, 0)]
PLANE = ("y", "x")


def pack(gate, up, down):
    last = jnp.pad(down[:, 1536:], ((0, 0), (0, 256)))
    return jnp.concatenate([gate, up, down[:, :768], down[:, 768:1536], last], axis=0)


def unpack(full):
    count = full.shape[0]
    gate = full[:, :64].reshape(count * 64, 768)
    up = full[:, 64:128].reshape(count * 64, 768)
    down = jnp.concatenate([full[:, 128:152], full[:, 152:176], full[:, 176:, :512]], axis=2)
    return gate, up, down.reshape(count * 24, 2048)


def swap(block):
    moves = [(a * 4 + b, b * 4 + a) for a in range(4) for b in range(4)]
    return lax.ppermute(block, ("y", "zh"), moves)


def shards(tokens, out_grad, routes, route_probs, gate_weight, up_weight, down_weight):
    tok_count, model_width = tokens.shape
    top_count = routes.shape[1]
    experts = 16
    capacity = tok_count * top_count * 5 // (4 * experts)
    route_count = tok_count * top_count
    packed = pack(gate_weight[0], up_weight[0], down_weight[0])
    full = lax.all_gather(swap(packed), ("zh", "zl", "core"), axis=0)
    full = full.reshape(4, 4, 2, 200, 768).swapaxes(0, 1).reshape(32, 200, 768)
    flat_routes = routes.reshape(route_count)
    onehot = (flat_routes[:, None] == jnp.arange(experts, dtype=jnp.int32)[None, :]).astype(
        jnp.int32
    )
    slot_index = jnp.sum((jnp.cumsum(onehot, axis=0) - onehot) * onehot, axis=1)
    target = flat_routes * capacity + slot_index
    token_rows = jnp.repeat(tokens, top_count, axis=0)
    grad_rows = (
        route_probs.reshape(route_count)[:, None]
        * jnp.repeat(out_grad, top_count, axis=0).astype(jnp.float32)
    ).astype(jnp.bfloat16)
    sent = flat_routes * (2 * capacity) + slot_index
    buffer = jnp.zeros((experts * 2 * capacity, model_width), jnp.bfloat16)
    buffer = buffer.at[sent].set(token_rows).at[sent + capacity].set(grad_rows)
    recv = lax.all_to_all(
        buffer.reshape(experts, 2 * capacity, model_width),
        PLANE,
        split_axis=0,
        concat_axis=0,
        tiled=True,
    )
    token_in = recv[:, :capacity].reshape(experts * capacity, model_width)
    grad_in = recv[:, capacity:].reshape(experts * capacity, model_width)
    gate_mat, up_mat, down_mat = unpack(full)
    gate_pre = jnp.dot(token_in, gate_mat, preferred_element_type=jnp.float32)
    up_pre = jnp.dot(token_in, up_mat, preferred_element_type=jnp.float32)
    sigmoid_gate = jax.nn.sigmoid(gate_pre)
    hidden = (gate_pre * sigmoid_gate * up_pre).astype(jnp.bfloat16)
    weight_term = lax.dot_general(
        hidden, grad_in, (((0,), (0,)), ((), ())), preferred_element_type=jnp.float32
    )
    terms = weight_term.astype(jnp.bfloat16).reshape(16, 2, 24, 2048)
    core = lax.axis_index("core")
    kept = lax.dynamic_index_in_dim(terms, core, 1, keepdims=False)
    given = lax.dynamic_index_in_dim(terms, 1 - core, 1, keepdims=False)
    given = lax.ppermute(given, "core", SWAP_CORES)
    both = (kept.astype(jnp.float32) + given.astype(jnp.float32)).astype(jnp.bfloat16)
    both = both.reshape(4, 4, 24, 2048).swapaxes(0, 1).reshape(16, 24, 2048)
    shard_grad = lax.psum_scatter(both, ("zh", "zl"), scatter_dimension=0, tiled=True)
    shard_grad = swap(shard_grad)
    hidden_grad = lax.dot_general(
        grad_in, down_mat, (((1,), (1,)), ((), ())), preferred_element_type=jnp.float32
    )
    gate_grad = (
        hidden_grad * up_pre * sigmoid_gate * (1.0 + gate_pre * (1.0 - sigmoid_gate))
    ).astype(jnp.bfloat16)
    up_grad = (hidden_grad * gate_pre * sigmoid_gate).astype(jnp.bfloat16)
    input_grad = lax.dot_general(
        gate_grad, gate_mat, (((1,), (1,)), ((), ())), preferred_element_type=jnp.float32
    )
    input_grad = input_grad + lax.dot_general(
        up_grad, up_mat, (((1,), (1,)), ((), ())), preferred_element_type=jnp.float32
    )
    input_grad = input_grad.astype(jnp.bfloat16)
    returned = lax.all_to_all(
        input_grad.reshape(experts, capacity, model_width),
        PLANE,
        split_axis=0,
        concat_axis=0,
        tiled=True,
    )
    route_grads = returned.reshape(experts * capacity, model_width)[target]
    token_grad = jnp.sum(
        route_grads.astype(jnp.float32).reshape(tok_count, top_count, model_width), axis=1
    ).astype(jnp.bfloat16)
    return (token_grad, shard_grad.astype(jnp.float32).reshape(1, 24, 2048))


def solution(mesh):
    fine = Mesh(mesh.devices.reshape(SIZES), AXES)
    rows, experts, parts = AXES, ("zh", "x"), ("zl", "y", "core")
    in_specs = (
        P(rows, None),
        P(rows, None),
        P(rows, None),
        P(rows, None),
        P(experts, parts, None),
        P(experts, parts, None),
        P(experts, parts, None),
    )
    out_specs = (P(rows, None), P(experts, parts, None))
    return jax.shard_map(shards, mesh=fine, in_specs=in_specs, out_specs=out_specs, check_vma=False)
```

```python
import jax
import jax.numpy as jnp
from jax import lax
from jax.experimental import pallas as pl
from jax.experimental.pallas import tpu as pltpu
from jax.sharding import Mesh, PartitionSpec as P

AXES = ("zl", "y", "core", "zh", "x")
SIZES = (4, 4, 2, 4, 4)
SWAP_CORES = [(0, 1), (1, 0)]
PLANE = ("y", "x")


STEP_A = ((0, 2, 0, 2), (2, 0, 2, 0), (1, 1, 1, 1), (3, 3, 3, 3))
STEP_B = ((0, 2, 0, 2), (2, 0, 2, 0), (3, 3, 3, 3), (1, 1, 1, 1))
Z = ("zl", "zh")


def swap(block, step):
    moves = [(y * 4 + e, e * 4 + (e + step[y][e]) % 4) for y in range(4) for e in range(4)]
    return lax.ppermute(block, ("y", "zh"), moves)


def came_from(step):
    table = [[0] * 4 for _ in range(4)]
    for y in range(4):
        for e in range(4):
            table[e][(e + step[y][e]) % 4] = y
    return jnp.array(table, jnp.int32)


def went_to(step):
    return jnp.array([[(e + step[y][e]) % 4 for y in range(4)] for e in range(4)], jnp.int32)


def along_z(block, by):
    place = lambda z: (z % 4) * 4 + (z // 4) % 4
    return lax.ppermute(block, Z, [(place(z), place(z + by)) for z in range(16)])


def turn(x, by):
    return lax.dynamic_slice_in_dim(jnp.concatenate([x, x], axis=0), by % 4, 4, axis=0)


def add(a, b):
    return (a.astype(jnp.float32) + b.astype(jnp.float32)).astype(jnp.bfloat16)


def forward_kernel(info, tok, grad, full, kept, given, gate_pre, up_pre, gate_out, up_out, gate, up, sems):
    for part, (buffer, first) in enumerate(((gate, 0), (up, 64))):
        for w in range(4):
            pltpu.make_async_copy(
                full.at[w, :, :, pl.ds(first, 64), :], buffer.at[:, info[w]], sems.at[part, w]
            ).start()
    pre = []
    for part, (buffer, first, out) in enumerate(((gate, 0, gate_out), (up, 64, up_out))):
        for w in range(4):
            pltpu.make_async_copy(
                full.at[w, :, :, pl.ds(first, 64), :], buffer.at[:, info[w]], sems.at[part, w]
            ).wait()
        pltpu.make_async_copy(buffer, out, sems.at[2, part]).start()
        pre.append(
            jnp.dot(tok[...], buffer[...].reshape(2048, 768), preferred_element_type=jnp.float32)
        )
    gate_pre[...], up_pre[...] = pre
    hidden = pre[0] * jax.nn.sigmoid(pre[0]) * pre[1]
    turned = hidden.astype(jnp.bfloat16).astype(jnp.float32).T.reshape(16, 2, 24, 320)
    mine = info[4] == 0
    for out, even in ((kept, mine), (given, jnp.logical_not(mine))):
        rows = jnp.where(even, turned[:, 0], turned[:, 1]).reshape(384, 320)
        out[...] = jnp.dot(
            rows.astype(jnp.bfloat16), grad[...], preferred_element_type=jnp.float32
        ).astype(jnp.bfloat16)
    pltpu.make_async_copy(gate, gate_out, sems.at[2, 0]).wait()
    pltpu.make_async_copy(up, up_out, sems.at[2, 1]).wait()


def forward(info, tok, grad, full):
    f32, b16 = jnp.float32, jnp.bfloat16
    whole = pl.BlockSpec(memory_space=pltpu.VMEM)
    far = pl.BlockSpec(memory_space=pl.ANY)
    mats = (4, 4, 2, 64, 768)
    return pl.pallas_call(
        forward_kernel,
        out_shape=(
            jax.ShapeDtypeStruct((384, 2048), b16),
            jax.ShapeDtypeStruct((384, 2048), b16),
            jax.ShapeDtypeStruct((320, 768), f32),
            jax.ShapeDtypeStruct((320, 768), f32),
            jax.ShapeDtypeStruct(mats, b16),
            jax.ShapeDtypeStruct(mats, b16),
        ),
        in_specs=[pl.BlockSpec(memory_space=pltpu.SMEM), whole, whole, far],
        out_specs=(whole, whole, whole, whole, far, far),
        scratch_shapes=[
            pltpu.VMEM(mats, b16),
            pltpu.VMEM(mats, b16),
            pltpu.SemaphoreType.DMA((3, 4)),
        ],
        compiler_params=pltpu.CompilerParams(vmem_limit_bytes=48 * 1024 * 1024),
        cost_estimate=pl.CostEstimate(
            flops=3 * 2 * 320 * 2048 * 768, bytes_accessed=24_000_000, transcendentals=320 * 768
        ),
    )(info, tok, grad, full)


def scatter_sum(kept, given):
    zl = lax.axis_index("zl")
    total = add(kept, lax.ppermute(given, "core", SWAP_CORES))
    total = turn(total, zl)
    half = 1024
    low = along_z(total[2][..., :half], 1)
    high = along_z(total[2][..., half:], -1)
    up = jnp.concatenate([add(total[1][..., :half], low), total[1][..., half:]], axis=-1)
    down = jnp.concatenate([total[3][..., :half], add(total[3][..., half:], high)], axis=-1)
    from_low = along_z(up, 1)
    from_high = along_z(down, -1)
    total = total[0].astype(jnp.float32) + from_low.astype(jnp.float32)
    total = (total + from_high.astype(jnp.float32)).astype(jnp.bfloat16)
    total = lax.all_to_all(total, "y", split_axis=0, concat_axis=0, tiled=True)
    total = lax.all_to_all(total, "zh", split_axis=0, concat_axis=0, tiled=True)
    return jnp.sum(total.astype(jnp.float32), axis=0)


def shards(tokens, out_grad, routes, route_probs, gate_weight, up_weight, down_weight):
    tok_count, model_width = tokens.shape
    top_count = routes.shape[1]
    experts = 16
    capacity = tok_count * top_count * 5 // (4 * experts)
    route_count = tok_count * top_count
    y = lax.axis_index("y")
    down = down_weight[0]
    last = jnp.pad(down[:, 1536:], ((0, 0), (0, 256)))
    part_a = swap(jnp.concatenate([gate_weight[0], up_weight[0]], axis=0), STEP_A)
    part_b = swap(jnp.concatenate([down[:, :768], down[:, 768:1536], last], axis=0), STEP_B)
    packed = jnp.concatenate([part_a, part_b], axis=0)
    full = lax.all_gather(packed, ("zh", "zl", "core"), axis=0).reshape(4, 4, 2, 200, 768)
    flat_routes = routes.reshape(route_count)
    onehot = (flat_routes[:, None] == jnp.arange(experts, dtype=jnp.int32)[None, :]).astype(
        jnp.int32
    )
    slot_index = jnp.sum((jnp.cumsum(onehot, axis=0) - onehot) * onehot, axis=1)
    target = flat_routes * capacity + slot_index
    token_rows = jnp.repeat(tokens, top_count, axis=0)
    grad_rows = (
        route_probs.reshape(route_count)[:, None]
        * jnp.repeat(out_grad, top_count, axis=0).astype(jnp.float32)
    ).astype(jnp.bfloat16)
    sent = flat_routes * (2 * capacity) + slot_index
    buffer = jnp.zeros((experts * 2 * capacity, model_width), jnp.bfloat16)
    buffer = buffer.at[sent].set(token_rows).at[sent + capacity].set(grad_rows)
    recv = lax.all_to_all(
        buffer.reshape(experts, 2 * capacity, model_width),
        PLANE,
        split_axis=0,
        concat_axis=0,
        tiled=True,
    )
    token_in = recv[:, :capacity].reshape(experts * capacity, model_width)
    grad_in = recv[:, capacity:].reshape(experts * capacity, model_width)
    info = jnp.concatenate([came_from(STEP_A)[y], lax.axis_index("core")[None].astype(jnp.int32)])
    kept, given, gate_pre, up_pre, gate_mat, up_mat = forward(info, token_in, grad_in, full)
    shard_grad = scatter_sum(kept.reshape(4, 4, 24, 2048), given.reshape(4, 4, 24, 2048))
    gate_mat, up_mat = gate_mat.reshape(2048, 768), up_mat.reshape(2048, 768)
    sigmoid_gate = jax.nn.sigmoid(gate_pre)
    spread = jnp.concatenate(
        [full[..., 128:152, :], full[..., 152:176, :], full[..., 176:, :512]], axis=-1
    )
    places = went_to(STEP_B)[y]
    down_mat = jnp.stack(
        [lax.dynamic_index_in_dim(spread, places[k], 0, keepdims=False) for k in range(4)], axis=1
    ).reshape(768, 2048)
    hidden_grad = lax.dot_general(
        grad_in, down_mat, (((1,), (1,)), ((), ())), preferred_element_type=jnp.float32
    )
    gate_grad = (
        hidden_grad * up_pre * sigmoid_gate * (1.0 + gate_pre * (1.0 - sigmoid_gate))
    ).astype(jnp.bfloat16)
    up_grad = (hidden_grad * gate_pre * sigmoid_gate).astype(jnp.bfloat16)
    input_grad = lax.dot_general(
        gate_grad, gate_mat, (((1,), (1,)), ((), ())), preferred_element_type=jnp.float32
    )
    input_grad = input_grad + lax.dot_general(
        up_grad, up_mat, (((1,), (1,)), ((), ())), preferred_element_type=jnp.float32
    )
    input_grad = input_grad.astype(jnp.bfloat16)
    returned = lax.all_to_all(
        input_grad.reshape(experts, capacity, model_width),
        PLANE,
        split_axis=0,
        concat_axis=0,
        tiled=True,
    )
    route_grads = returned.reshape(experts * capacity, model_width)[target]
    token_grad = jnp.sum(
        route_grads.astype(jnp.float32).reshape(tok_count, top_count, model_width), axis=1
    ).astype(jnp.bfloat16)
    return (token_grad, shard_grad.reshape(1, 24, 2048))


def solution(mesh):
    fine = Mesh(mesh.devices.reshape(SIZES), AXES)
    rows, experts, parts = AXES, ("zh", "x"), ("zl", "y", "core")
    in_specs = (
        P(rows, None),
        P(rows, None),
        P(rows, None),
        P(rows, None),
        P(experts, parts, None),
        P(experts, parts, None),
        P(experts, parts, None),
    )
    out_specs = (P(rows, None), P(experts, parts, None))
    return jax.shard_map(shards, mesh=fine, in_specs=in_specs, out_specs=out_specs, check_vma=False)
```

```python
import jax
import jax.numpy as jnp
from jax import lax
from jax.experimental import pallas as pl
from jax.experimental.pallas import tpu as pltpu
from jax.sharding import Mesh, PartitionSpec as P

AXES = ("zl", "y", "core", "zh", "x")
SIZES = (4, 4, 2, 4, 4)
SWAP_CORES = [(0, 1), (1, 0)]
PLANE = ("y", "x")


STEP_A = ((2, 0, 2, 0), (1, 1, 1, 1), (0, 2, 0, 2), (3, 3, 3, 3))
STEP_B = ((2, 0, 2, 0), (3, 3, 3, 3), (0, 2, 0, 2), (1, 1, 1, 1))
Z = ("zl", "zh")


def swap(block, step):
    moves = [(y * 4 + e, e * 4 + (e + step[y][e]) % 4) for y in range(4) for e in range(4)]
    return lax.ppermute(block, ("y", "zh"), moves)


def came_from(step):
    table = [[0] * 4 for _ in range(4)]
    for y in range(4):
        for e in range(4):
            table[e][(e + step[y][e]) % 4] = y
    return jnp.array(table, jnp.int32)


def went_to(step):
    return jnp.array([[(e + step[y][e]) % 4 for y in range(4)] for e in range(4)], jnp.int32)


def along_z(block, by):
    place = lambda z: (z % 4) * 4 + (z // 4) % 4
    return lax.ppermute(block, Z, [(place(z), place(z + by)) for z in range(16)])


def forward_kernel(
    info, tok, tok_far, grad, grad_far, full, p0, p1, low, high, p3, gate_pre, up_pre, gate_out, up_out,
    gate, up, rows, sems,
):
    def load(part, buffer, w):
        block = full.at[w, :, :, pl.ds(part * 64, 64), :]
        return pltpu.make_async_copy(block, buffer.at[:, info[w]], sems.at[part, w])

    for part, buffer in enumerate((gate, up)):
        for w in range(4):
            load(part, buffer, w).start()
    pre = []
    for part, (buffer, out) in enumerate(((gate, gate_out), (up, up_out))):
        for w in range(4):
            load(part, buffer, w).wait()
        pltpu.make_async_copy(buffer, out, sems.at[2, part]).start()
        mat = buffer[...].reshape(2048, 768)
        pre.append(
            [jnp.dot(t[...], mat, preferred_element_type=jnp.float32) for t in (tok, tok_far)]
        )
    gate_pre[...], up_pre[...] = pre[0][0], pre[1][0]
    for k in range(2):
        hidden = pre[0][k] * jax.nn.sigmoid(pre[0][k]) * pre[1][k]
        turned = hidden.astype(jnp.bfloat16).astype(jnp.float32).T
        rows[k] = turned.reshape(4, 4, 2, 24, 320)
    for k, outs in ((2, (low, high)), (1, (p1,)), (3, (p3,)), (0, (p0,))):
        total = 0.0
        for source, g in ((0, grad), (1, grad_far)):
            zl = lax.rem(info[5] + k, 4)
            mine = rows[source, zl, :, info[4]].reshape(96, 320).astype(jnp.bfloat16)
            total += jnp.dot(mine, g[...], preferred_element_type=jnp.float32)
        total = total.astype(jnp.bfloat16)
        width = 2048 // len(outs)
        for n, out in enumerate(outs):
            out[...] = total[:, n * width : (n + 1) * width]
    pltpu.make_async_copy(gate, gate_out, sems.at[2, 0]).wait()
    pltpu.make_async_copy(up, up_out, sems.at[2, 1]).wait()


def forward(info, tok, tok_far, grad, grad_far, full):
    f32, b16 = jnp.float32, jnp.bfloat16
    whole = pl.BlockSpec(memory_space=pltpu.VMEM)
    far = pl.BlockSpec(memory_space=pl.ANY)
    mats = (4, 4, 2, 64, 768)
    shape = jax.ShapeDtypeStruct
    piece, part = shape((96, 2048), b16), shape((96, 1024), b16)
    pre = shape((320, 768), f32)
    return pl.pallas_call(
        forward_kernel,
        out_shape=(piece, piece, part, part, piece, pre, pre, shape(mats, b16), shape(mats, b16)),
        in_specs=[pl.BlockSpec(memory_space=pltpu.SMEM)] + [whole] * 4 + [far],
        out_specs=(whole,) * 7 + (far,) * 2,
        scratch_shapes=[
            pltpu.VMEM(mats, b16),
            pltpu.VMEM(mats, b16),
            pltpu.VMEM((2, 4, 4, 2, 24, 320), f32),
            pltpu.SemaphoreType.DMA((3, 4)),
        ],
        compiler_params=pltpu.CompilerParams(vmem_limit_bytes=48 * 1024 * 1024),
        cost_estimate=pl.CostEstimate(
            flops=5 * 2 * 320 * 2048 * 768, bytes_accessed=24_000_000, transcendentals=640 * 768
        ),
    )(info, tok, tok_far, grad, grad_far, full)


def sum_zh(total):
    f32 = jnp.float32
    zh = lax.axis_index("zh")
    total = lax.dynamic_slice_in_dim(jnp.concatenate([total, total], axis=0), zh, 4, axis=0)
    moved = [
        lax.ppermute(total[k], "zh", [(a, (a + k) % 4) for a in range(4)]).astype(f32)
        for k in (1, 3, 2)
    ]
    return total[0].astype(f32) + moved[0] + moved[1] + moved[2]


def shards(tokens, out_grad, routes, route_probs, gate_weight, up_weight, down_weight):
    tok_count, model_width = tokens.shape
    top_count = routes.shape[1]
    experts = 16
    capacity = tok_count * top_count * 5 // (4 * experts)
    y = lax.axis_index("y")
    down = down_weight[0]
    last = jnp.pad(down[:, 1536:], ((0, 0), (0, 256)))
    part_a = swap(jnp.concatenate([gate_weight[0], up_weight[0]], axis=0), STEP_A)
    part_b = swap(jnp.concatenate([down[:, :768], down[:, 768:1536], last], axis=0), STEP_B)
    packed = jnp.concatenate([part_a, part_b], axis=0)
    full = lax.all_gather(packed, ("zh", "zl", "core"), axis=0).reshape(4, 4, 2, 200, 768)
    f32, b16 = jnp.float32, jnp.bfloat16
    named = routes[:, :, None] == jnp.arange(experts, dtype=jnp.int32)[None, None, :]
    names = jnp.any(named, axis=1)
    earlier = jnp.tril(jnp.ones((tok_count, tok_count), b16), -1)
    place = jnp.dot(earlier, names.astype(b16), preferred_element_type=f32)
    place = jnp.where(names, place, -1.0).T
    probs = jnp.sum(jnp.where(named, route_probs[:, :, None], 0.0), axis=1).T
    slots = jnp.arange(2 * capacity, dtype=jnp.int32)
    chosen = place[:, None, :] == (slots % capacity).astype(f32)[None, :, None]
    is_token = (slots < capacity)[None, :, None]
    scale = jnp.sum(jnp.where(chosen, probs[:, None, :], 0.0), axis=2)
    flat = (experts * 2 * capacity, tok_count)
    pick_token = (chosen & is_token).astype(b16).reshape(flat)
    pick_grad = (chosen & ~is_token).astype(b16).reshape(flat)
    buffer = jnp.dot(pick_token, tokens, preferred_element_type=f32)
    buffer += scale.reshape(-1, 1) * jnp.dot(pick_grad, out_grad, preferred_element_type=f32)
    buffer = buffer.astype(b16)
    slots = jnp.arange(capacity, dtype=jnp.int32).astype(f32)
    combine = (place[:, None, :] == slots[None, :, None]).astype(b16)
    combine = combine.reshape(experts * capacity, tok_count)
    recv = lax.all_to_all(
        buffer.reshape(experts, 2 * capacity, model_width),
        PLANE,
        split_axis=0,
        concat_axis=0,
        tiled=True,
    )
    rows_far = lax.ppermute(recv, "core", SWAP_CORES)
    flat = (experts * capacity, model_width)
    token_in, token_far = (r[:, :capacity].reshape(flat) for r in (recv, rows_far))
    grad_in, grad_far = (r[:, capacity:].reshape(flat) for r in (recv, rows_far))
    info = jnp.concatenate(
        [came_from(STEP_A)[y], jnp.stack([lax.axis_index("core"), lax.axis_index("zl")])]
    )
    out = forward(info, token_in, token_far, grad_in, grad_far, full)
    p0, p1, low, high, p3 = (piece.reshape(4, 24, -1) for piece in out[:5])
    p1, p3, low, high = along_z(p1, 1), along_z(p3, -1), along_z(low, 2), along_z(high, -2)
    gate_pre, up_pre, gate_mat, up_mat = out[5:]
    full, gate_pre = lax.optimization_barrier((full, gate_pre))
    gate_mat, up_mat = gate_mat.reshape(2048, 768), up_mat.reshape(2048, 768)
    sigmoid_gate = jax.nn.sigmoid(gate_pre)
    spread = jnp.concatenate(
        [full[..., 128:152, :], full[..., 152:176, :], full[..., 176:, :512]], axis=-1
    )
    places = went_to(STEP_B)[y]
    down_mat = jnp.stack(
        [lax.dynamic_index_in_dim(spread, places[k], 0, keepdims=False) for k in range(4)], axis=1
    ).reshape(768, 2048)
    hidden_grad = lax.dot_general(
        grad_in, down_mat, (((1,), (1,)), ((), ())), preferred_element_type=jnp.float32
    )
    gate_grad = (
        hidden_grad * up_pre * sigmoid_gate * (1.0 + gate_pre * (1.0 - sigmoid_gate))
    ).astype(jnp.bfloat16)
    up_grad = (hidden_grad * gate_pre * sigmoid_gate).astype(jnp.bfloat16)
    input_grad = lax.dot_general(
        gate_grad, gate_mat, (((1,), (1,)), ((), ())), preferred_element_type=jnp.float32
    )
    input_grad = input_grad + lax.dot_general(
        up_grad, up_mat, (((1,), (1,)), ((), ())), preferred_element_type=jnp.float32
    )
    input_grad = input_grad.astype(jnp.bfloat16)
    p1, p3, low, high, input_grad = lax.optimization_barrier((p1, p3, low, high, input_grad))
    far = jnp.concatenate([low, high], axis=-1).astype(f32)
    total = (p0.astype(f32) + p1.astype(f32) + p3.astype(f32) + far).astype(b16)
    total = lax.all_to_all(total, "y", split_axis=0, concat_axis=0, tiled=True)
    total, input_grad = lax.optimization_barrier((total, input_grad))
    shard_grad = sum_zh(total)
    returned = lax.all_to_all(
        input_grad.reshape(experts, capacity, model_width),
        PLANE,
        split_axis=0,
        concat_axis=0,
        tiled=True,
    )
    token_grad = lax.dot_general(
        combine,
        returned.reshape(experts * capacity, model_width),
        (((0,), (0,)), ((), ())),
        preferred_element_type=f32,
    ).astype(b16)
    return (token_grad, shard_grad.reshape(1, 24, 2048))


def solution(mesh):
    fine = Mesh(mesh.devices.reshape(SIZES), AXES)
    rows, experts, parts = AXES, ("zh", "x"), ("zl", "y", "core")
    in_specs = (
        P(rows, None),
        P(rows, None),
        P(rows, None),
        P(rows, None),
        P(experts, parts, None),
        P(experts, parts, None),
        P(experts, parts, None),
    )
    out_specs = (P(rows, None), P(experts, parts, None))
    return jax.shard_map(shards, mesh=fine, in_specs=in_specs, out_specs=out_specs, check_vma=False)
```

```python
import jax
import jax.numpy as jnp
from jax import lax
from jax.experimental import pallas as pl
from jax.experimental.pallas import tpu as pltpu
from jax.sharding import Mesh, PartitionSpec as P

AXES = ("zl", "y", "core", "zh", "x")
SIZES = (4, 4, 2, 4, 4)
SWAP_CORES = [(0, 1), (1, 0)]
PLANE = ("y", "x")


STEP_A = ((2, 0, 2, 0), (1, 1, 1, 1), (0, 2, 0, 2), (3, 3, 3, 3))
STEP_B = ((2, 0, 2, 0), (3, 3, 3, 3), (0, 2, 0, 2), (1, 1, 1, 1))
Z = ("zl", "zh")


def swap(block, step):
    moves = [(y * 4 + e, e * 4 + (e + step[y][e]) % 4) for y in range(4) for e in range(4)]
    return lax.ppermute(block, ("y", "zh"), moves)


def came_from(step):
    table = [[0] * 4 for _ in range(4)]
    for y in range(4):
        for e in range(4):
            table[e][(e + step[y][e]) % 4] = y
    return jnp.array(table, jnp.int32)


def went_to(step):
    return jnp.array([[(e + step[y][e]) % 4 for y in range(4)] for e in range(4)], jnp.int32)


def along_z(block, by):
    place = lambda z: (z % 4) * 4 + (z // 4) % 4
    return lax.ppermute(block, Z, [(place(z), place(z + by)) for z in range(16)])


def forward_kernel(
    info, tok, grad, full, p0, p1, low, high, p3, gate_pre, up_pre, gate_out, up_out,
    gate, up, rows, sems,
):
    def load(part, buffer, w):
        block = full.at[w, :, :, pl.ds(part * 64, 64), :]
        return pltpu.make_async_copy(block, buffer.at[:, info[w]], sems.at[part, w])

    for part, buffer in enumerate((gate, up)):
        for w in range(4):
            load(part, buffer, w).start()
    pre = []
    for part, (buffer, out) in enumerate(((gate, gate_out), (up, up_out))):
        for w in range(4):
            load(part, buffer, w).wait()
        pltpu.make_async_copy(buffer, out, sems.at[2, part]).start()
        mat = buffer[...].reshape(2048, 768)
        pre.append(jnp.dot(tok[...], mat, preferred_element_type=jnp.float32))
    gate_pre[...], up_pre[...] = pre[0][:320], pre[1][:320]
    hidden = pre[0] * jax.nn.sigmoid(pre[0]) * pre[1]
    rows[...] = hidden.astype(jnp.bfloat16).astype(jnp.float32).T.reshape(4, 4, 2, 24, 640)
    mine = [rows[lax.rem(info[5] + k, 4), :, info[4]].reshape(96, 640) for k in range(4)]
    mine = jnp.concatenate(mine, axis=0).astype(jnp.bfloat16)
    total = jnp.dot(mine, grad[...], preferred_element_type=jnp.float32).astype(jnp.bfloat16)
    p0[...], p1[...], p3[...] = total[:96], total[96:192], total[288:]
    low[...], high[...] = total[192:288, :1024], total[192:288, 1024:]
    pltpu.make_async_copy(gate, gate_out, sems.at[2, 0]).wait()
    pltpu.make_async_copy(up, up_out, sems.at[2, 1]).wait()


def forward(info, tok, grad, full):
    f32, b16 = jnp.float32, jnp.bfloat16
    whole = pl.BlockSpec(memory_space=pltpu.VMEM)
    far = pl.BlockSpec(memory_space=pl.ANY)
    mats = (4, 4, 2, 64, 768)
    shape = jax.ShapeDtypeStruct
    piece, part = shape((96, 2048), b16), shape((96, 1024), b16)
    pre = shape((320, 768), f32)
    return pl.pallas_call(
        forward_kernel,
        out_shape=(piece, piece, part, part, piece, pre, pre, shape(mats, b16), shape(mats, b16)),
        in_specs=[pl.BlockSpec(memory_space=pltpu.SMEM), whole, whole, far],
        out_specs=(whole,) * 7 + (far,) * 2,
        scratch_shapes=[
            pltpu.VMEM(mats, b16),
            pltpu.VMEM(mats, b16),
            pltpu.VMEM((4, 4, 2, 24, 640), f32),
            pltpu.SemaphoreType.DMA((3, 4)),
        ],
        compiler_params=pltpu.CompilerParams(vmem_limit_bytes=48 * 1024 * 1024),
        cost_estimate=pl.CostEstimate(
            flops=5 * 2 * 320 * 2048 * 768, bytes_accessed=24_000_000, transcendentals=640 * 768
        ),
    )(info, tok, grad, full)


def sum_zh(total):
    f32 = jnp.float32
    zh = lax.axis_index("zh")
    total = lax.dynamic_slice_in_dim(jnp.concatenate([total, total], axis=0), zh, 4, axis=0)
    moved = [
        lax.ppermute(total[k], "zh", [(a, (a + k) % 4) for a in range(4)]).astype(f32)
        for k in (1, 3, 2)
    ]
    return total[0].astype(f32) + moved[0] + moved[1] + moved[2]


def shards(tokens, out_grad, routes, route_probs, gate_weight, up_weight, down_weight):
    tok_count, model_width = tokens.shape
    top_count = routes.shape[1]
    experts = 16
    capacity = tok_count * top_count * 5 // (4 * experts)
    y = lax.axis_index("y")
    down = down_weight[0]
    last = jnp.pad(down[:, 1536:], ((0, 0), (0, 256)))
    part_a = swap(jnp.concatenate([gate_weight[0], up_weight[0]], axis=0), STEP_A)
    part_b = swap(jnp.concatenate([down[:, :768], down[:, 768:1536], last], axis=0), STEP_B)
    packed = jnp.concatenate([part_a, part_b], axis=0)
    full = lax.all_gather(packed, ("zh", "zl", "core"), axis=0).reshape(4, 4, 2, 200, 768)
    f32, b16 = jnp.float32, jnp.bfloat16
    named = routes[:, :, None] == jnp.arange(experts, dtype=jnp.int32)[None, None, :]
    names = jnp.any(named, axis=1)
    earlier = jnp.tril(jnp.ones((tok_count, tok_count), b16), -1)
    place = jnp.dot(earlier, names.astype(b16), preferred_element_type=f32)
    place = jnp.where(names, place, -1.0).T
    probs = jnp.sum(jnp.where(named, route_probs[:, :, None], 0.0), axis=1).T
    slots = jnp.arange(2 * capacity, dtype=jnp.int32)
    chosen = place[:, None, :] == (slots % capacity).astype(f32)[None, :, None]
    is_token = (slots < capacity)[None, :, None]
    scale = jnp.sum(jnp.where(chosen, probs[:, None, :], 0.0), axis=2)
    flat = (experts * 2 * capacity, tok_count)
    pick_token = (chosen & is_token).astype(b16).reshape(flat)
    pick_grad = (chosen & ~is_token).astype(b16).reshape(flat)
    buffer = jnp.dot(pick_token, tokens, preferred_element_type=f32)
    buffer += scale.reshape(-1, 1) * jnp.dot(pick_grad, out_grad, preferred_element_type=f32)
    buffer = buffer.astype(b16)
    slots = jnp.arange(capacity, dtype=jnp.int32).astype(f32)
    combine = (place[:, None, :] == slots[None, :, None]).astype(b16)
    combine = combine.reshape(experts * capacity, tok_count)
    recv = lax.all_to_all(
        buffer.reshape(experts, 2 * capacity, model_width),
        PLANE,
        split_axis=0,
        concat_axis=0,
        tiled=True,
    )
    rows_far = lax.ppermute(recv, "core", SWAP_CORES)
    flat = (2 * experts * capacity, model_width)
    token_in = jnp.concatenate([recv[:, :capacity], rows_far[:, :capacity]], axis=0).reshape(flat)
    grad_all = jnp.concatenate([recv[:, capacity:], rows_far[:, capacity:]], axis=0).reshape(flat)
    grad_in = grad_all[: experts * capacity]
    info = jnp.concatenate(
        [came_from(STEP_A)[y], jnp.stack([lax.axis_index("core"), lax.axis_index("zl")])]
    )
    out = forward(info, token_in, grad_all, full)
    p0, p1, low, high, p3 = (piece.reshape(4, 24, -1) for piece in out[:5])
    p1, p3, low, high = along_z(p1, 1), along_z(p3, -1), along_z(low, 2), along_z(high, -2)
    gate_pre, up_pre, gate_mat, up_mat = out[5:]
    full, gate_pre = lax.optimization_barrier((full, gate_pre))
    gate_mat, up_mat = gate_mat.reshape(2048, 768), up_mat.reshape(2048, 768)
    sigmoid_gate = jax.nn.sigmoid(gate_pre)
    spread = jnp.concatenate(
        [full[..., 128:152, :], full[..., 152:176, :], full[..., 176:, :512]], axis=-1
    )
    places = went_to(STEP_B)[y]
    down_mat = jnp.stack(
        [lax.dynamic_index_in_dim(spread, places[k], 0, keepdims=False) for k in range(4)], axis=1
    ).reshape(768, 2048)
    hidden_grad = lax.dot_general(
        grad_in, down_mat, (((1,), (1,)), ((), ())), preferred_element_type=jnp.float32
    )
    gate_grad = (
        hidden_grad * up_pre * sigmoid_gate * (1.0 + gate_pre * (1.0 - sigmoid_gate))
    ).astype(jnp.bfloat16)
    up_grad = (hidden_grad * gate_pre * sigmoid_gate).astype(jnp.bfloat16)
    input_grad = lax.dot_general(
        gate_grad, gate_mat, (((1,), (1,)), ((), ())), preferred_element_type=jnp.float32
    )
    input_grad = input_grad + lax.dot_general(
        up_grad, up_mat, (((1,), (1,)), ((), ())), preferred_element_type=jnp.float32
    )
    input_grad = input_grad.astype(jnp.bfloat16)
    p1, p3, low, high, input_grad = lax.optimization_barrier((p1, p3, low, high, input_grad))
    far = jnp.concatenate([low, high], axis=-1).astype(f32)
    total = (p0.astype(f32) + p1.astype(f32) + p3.astype(f32) + far).astype(b16)
    total = lax.all_to_all(total, "y", split_axis=0, concat_axis=0, tiled=True)
    total, input_grad = lax.optimization_barrier((total, input_grad))
    shard_grad = sum_zh(total)
    returned = lax.all_to_all(
        input_grad.reshape(experts, capacity, model_width),
        PLANE,
        split_axis=0,
        concat_axis=0,
        tiled=True,
    )
    token_grad = lax.dot_general(
        combine,
        returned.reshape(experts * capacity, model_width),
        (((0,), (0,)), ((), ())),
        preferred_element_type=f32,
    ).astype(b16)
    return (token_grad, shard_grad.reshape(1, 24, 2048))


def solution(mesh):
    fine = Mesh(mesh.devices.reshape(SIZES), AXES)
    rows, experts, parts = AXES, ("zh", "x"), ("zl", "y", "core")
    in_specs = (
        P(rows, None),
        P(rows, None),
        P(rows, None),
        P(rows, None),
        P(experts, parts, None),
        P(experts, parts, None),
        P(experts, parts, None),
    )
    out_specs = (P(rows, None), P(experts, parts, None))
    return jax.shard_map(shards, mesh=fine, in_specs=in_specs, out_specs=out_specs, check_vma=False)
```

```python
import jax
import jax.numpy as jnp
from jax import lax
from jax.experimental import pallas as pl
from jax.experimental.pallas import tpu as pltpu
from jax.sharding import Mesh, PartitionSpec as P

AXES = ("zl", "y", "core", "zh", "x")
SIZES = (4, 4, 2, 4, 4)
SWAP_CORES = [(0, 1), (1, 0)]
PLANE = ("y", "x")


STEP_A = ((2, 0, 2, 0), (1, 1, 1, 1), (0, 2, 0, 2), (3, 3, 3, 3))
STEP_B = ((2, 0, 2, 0), (3, 3, 3, 3), (0, 2, 0, 2), (1, 1, 1, 1))
Z = ("zl", "zh")


def swap(block, step):
    moves = [(y * 4 + e, e * 4 + (e + step[y][e]) % 4) for y in range(4) for e in range(4)]
    return lax.ppermute(block, ("y", "zh"), moves)


def came_from(step):
    table = [[0] * 4 for _ in range(4)]
    for y in range(4):
        for e in range(4):
            table[e][(e + step[y][e]) % 4] = y
    return jnp.array(table, jnp.int32)


def went_to(step):
    return jnp.array([[(e + step[y][e]) % 4 for y in range(4)] for e in range(4)], jnp.int32)


def along_z(block, by):
    place = lambda z: (z % 4) * 4 + (z // 4) % 4
    return lax.ppermute(block, Z, [(place(z), place(z + by)) for z in range(16)])


def forward_kernel(
    info, tok, grad, full, p0, p1, low, high, p3, gate_pre, up_pre, gate_out, up_out,
    gate, up, rows, sems,
):
    def load(part, buffer, w):
        block = full.at[w, :, :, pl.ds(part * 64, 64), :]
        return pltpu.make_async_copy(block, buffer.at[:, info[w]], sems.at[part, w])

    for part, buffer in enumerate((gate, up)):
        for w in range(4):
            load(part, buffer, w).start()
    pre = []
    for part, (buffer, out) in enumerate(((gate, gate_out), (up, up_out))):
        for w in range(4):
            load(part, buffer, w).wait()
        pltpu.make_async_copy(buffer, out, sems.at[2, part]).start()
        mat = buffer[...].reshape(2048, 768)
        pre.append(jnp.dot(tok[...], mat, preferred_element_type=jnp.float32))
    gate_pre[...], up_pre[...] = pre[0][:320], pre[1][:320]
    hidden = pre[0] * jax.nn.sigmoid(pre[0]) * pre[1]
    rows[...] = hidden.astype(jnp.bfloat16).astype(jnp.float32).T.reshape(4, 4, 2, 24, 640)
    mine = [rows[lax.rem(info[5] + k, 4), :, info[4]].reshape(96, 640) for k in range(4)]
    mine = jnp.concatenate(mine, axis=0).astype(jnp.bfloat16)
    total = jnp.dot(mine, grad[...], preferred_element_type=jnp.float32).astype(jnp.bfloat16)
    p0[...], p1[...], p3[...] = total[:96], total[96:192], total[288:]
    low[...], high[...] = total[192:288, :1024], total[192:288, 1024:]
    pltpu.make_async_copy(gate, gate_out, sems.at[2, 0]).wait()
    pltpu.make_async_copy(up, up_out, sems.at[2, 1]).wait()


def forward(info, tok, grad, full):
    f32, b16 = jnp.float32, jnp.bfloat16
    whole = pl.BlockSpec(memory_space=pltpu.VMEM)
    far = pl.BlockSpec(memory_space=pl.ANY)
    mats = (4, 4, 2, 64, 768)
    shape = jax.ShapeDtypeStruct
    piece, part = shape((96, 2048), b16), shape((96, 1024), b16)
    pre = shape((320, 768), f32)
    return pl.pallas_call(
        forward_kernel,
        out_shape=(piece, piece, part, part, piece, pre, pre, shape(mats, b16), shape(mats, b16)),
        in_specs=[pl.BlockSpec(memory_space=pltpu.SMEM), whole, whole, far],
        out_specs=(whole,) * 7 + (far,) * 2,
        scratch_shapes=[
            pltpu.VMEM(mats, b16),
            pltpu.VMEM(mats, b16),
            pltpu.VMEM((4, 4, 2, 24, 640), f32),
            pltpu.SemaphoreType.DMA((3, 4)),
        ],
        compiler_params=pltpu.CompilerParams(vmem_limit_bytes=48 * 1024 * 1024),
        cost_estimate=pl.CostEstimate(
            flops=5 * 2 * 320 * 2048 * 768, bytes_accessed=24_000_000, transcendentals=640 * 768
        ),
    )(info, tok, grad, full)


def sum_zh(total):
    f32 = jnp.float32
    zh = lax.axis_index("zh")
    total = lax.dynamic_slice_in_dim(jnp.concatenate([total, total], axis=0), zh, 4, axis=0)
    moved = [
        lax.ppermute(total[k], "zh", [(a, (a + k) % 4) for a in range(4)]).astype(f32)
        for k in (1, 3, 2)
    ]
    return total[0].astype(f32) + moved[0] + moved[1] + moved[2]


def shards(tokens, out_grad, routes, route_probs, gate_weight, up_weight, down_weight):
    tok_count, model_width = tokens.shape
    top_count = routes.shape[1]
    experts = 16
    capacity = tok_count * top_count * 5 // (4 * experts)
    y = lax.axis_index("y")
    down = down_weight[0]
    last = jnp.pad(down[:, 1536:], ((0, 0), (0, 256)))
    part_a = swap(jnp.concatenate([gate_weight[0], up_weight[0]], axis=0), STEP_A)
    part_b = swap(jnp.concatenate([down[:, :768], down[:, 768:1536], last], axis=0), STEP_B)
    packed = jnp.concatenate([part_a, part_b], axis=0)
    full = lax.all_gather(packed, ("zh", "zl", "core"), axis=0).reshape(4, 4, 2, 200, 768)
    f32, b16 = jnp.float32, jnp.bfloat16
    named = routes[:, :, None] == jnp.arange(experts, dtype=jnp.int32)[None, None, :]
    names = jnp.any(named, axis=1)
    earlier = jnp.tril(jnp.ones((tok_count, tok_count), b16), -1)
    place = jnp.dot(earlier, names.astype(b16), preferred_element_type=f32)
    place = jnp.where(names, place, -1.0).T
    probs = jnp.sum(jnp.where(named, route_probs[:, :, None], 0.0), axis=1).T
    slots = jnp.arange(2 * capacity, dtype=jnp.int32)
    chosen = place[:, None, :] == (slots % capacity).astype(f32)[None, :, None]
    is_token = (slots < capacity)[None, :, None]
    scale = jnp.sum(jnp.where(chosen, probs[:, None, :], 0.0), axis=2)
    flat = (experts * 2 * capacity, tok_count)
    pick_token = (chosen & is_token).astype(b16).reshape(flat)
    pick_grad = (chosen & ~is_token).astype(b16).reshape(flat)
    buffer = jnp.dot(pick_token, tokens, preferred_element_type=f32)
    buffer += scale.reshape(-1, 1) * jnp.dot(pick_grad, out_grad, preferred_element_type=f32)
    buffer = buffer.astype(b16)
    slots = jnp.arange(capacity, dtype=jnp.int32).astype(f32)
    combine = (place[:, None, :] == slots[None, :, None]).astype(b16)
    combine = combine.reshape(experts * capacity, tok_count)
    recv = lax.all_to_all(
        buffer.reshape(experts, 2 * capacity, model_width),
        PLANE,
        split_axis=0,
        concat_axis=0,
        tiled=True,
    )
    rows_far = lax.ppermute(recv, "core", SWAP_CORES)
    flat = (2 * experts * capacity, model_width)
    token_in = jnp.concatenate([recv[:, :capacity], rows_far[:, :capacity]], axis=0).reshape(flat)
    grad_all = jnp.concatenate([recv[:, capacity:], rows_far[:, capacity:]], axis=0).reshape(flat)
    grad_in = grad_all[: experts * capacity]
    info = jnp.concatenate(
        [came_from(STEP_A)[y], jnp.stack([lax.axis_index("core"), lax.axis_index("zl")])]
    )
    out = forward(info, token_in, grad_all, full)
    p0, p1, low, high, p3 = (piece.reshape(4, 24, -1) for piece in out[:5])
    p1, p3, low, high = along_z(p1, 1), along_z(p3, -1), along_z(low, 2), along_z(high, -2)
    gate_pre, up_pre, gate_mat, up_mat = out[5:]
    full, gate_pre = lax.optimization_barrier((full, gate_pre))
    gate_mat, up_mat = gate_mat.reshape(2048, 768), up_mat.reshape(2048, 768)
    sigmoid_gate = jax.nn.sigmoid(gate_pre)
    spread = jnp.concatenate(
        [full[..., 128:152, :], full[..., 152:176, :], full[..., 176:, :512]], axis=-1
    )
    places = went_to(STEP_B)[y]
    down_mat = jnp.stack(
        [lax.dynamic_index_in_dim(spread, places[k], 0, keepdims=False) for k in range(4)], axis=1
    ).reshape(768, 2048)
    hidden_grad = lax.dot_general(
        grad_in, down_mat, (((1,), (1,)), ((), ())), preferred_element_type=jnp.float32
    )
    gate_grad = (
        hidden_grad * up_pre * sigmoid_gate * (1.0 + gate_pre * (1.0 - sigmoid_gate))
    ).astype(jnp.bfloat16)
    up_grad = (hidden_grad * gate_pre * sigmoid_gate).astype(jnp.bfloat16)
    input_grad = lax.dot_general(
        gate_grad, gate_mat, (((1,), (1,)), ((), ())), preferred_element_type=jnp.float32
    )
    input_grad = input_grad + lax.dot_general(
        up_grad, up_mat, (((1,), (1,)), ((), ())), preferred_element_type=jnp.float32
    )
    input_grad = input_grad.astype(jnp.bfloat16)
    p1, p3, low, high, input_grad = lax.optimization_barrier((p1, p3, low, high, input_grad))
    far = jnp.concatenate([low, high], axis=-1).astype(f32)
    total = (p0.astype(f32) + p1.astype(f32) + p3.astype(f32) + far).astype(b16)
    total = lax.all_to_all(total, "y", split_axis=0, concat_axis=0, tiled=True)
    input_grad = input_grad.reshape(experts, capacity, model_width)
    total, input_grad = lax.optimization_barrier((total, input_grad))
    shard_grad = sum_zh(total)
    returned = lax.all_to_all(
        input_grad,
        PLANE,
        split_axis=0,
        concat_axis=0,
        tiled=True,
    )
    token_grad = lax.dot_general(
        combine,
        returned.reshape(experts * capacity, model_width),
        (((0,), (0,)), ((), ())),
        preferred_element_type=f32,
    ).astype(b16)
    return (token_grad, shard_grad.reshape(1, 24, 2048))


def solution(mesh):
    fine = Mesh(mesh.devices.reshape(SIZES), AXES)
    rows, experts, parts = AXES, ("zh", "x"), ("zl", "y", "core")
    in_specs = (
        P(rows, None),
        P(rows, None),
        P(rows, None),
        P(rows, None),
        P(experts, parts, None),
        P(experts, parts, None),
        P(experts, parts, None),
    )
    out_specs = (P(rows, None), P(experts, parts, None))
    return jax.shard_map(shards, mesh=fine, in_specs=in_specs, out_specs=out_specs, check_vma=False)
```
